32 devices in a mesh: groups: 2 (over y), context: 2 (over x), expert: 4 (over z), tensor: 2 (over core).
Axes of the slice: x: 2, y: 2, z: 4, core: 2. Of those that a mesh axis runs over, the one named last changes fastest.
Arguments:
- queries: bfloat16 [2048, 2048], P(('groups', 'context', 'expert'), 'tensor'), parts along dimension 0, may hold values from -60 to 60
- keys: bfloat16 [2048, 512], P(('groups', 'context', 'expert'), 'tensor'), parts along dimension 0, may hold values from -5 to 5
- values: bfloat16 [2048, 512], P(('groups', 'context', 'expert'), 'tensor'), parts along dimension 0, may hold values from -6 to 6
- resid: bfloat16 [2048, 2048], P(('groups', 'context', 'expert'), 'tensor'), parts along dimension 0, may hold values from -200 to 200
- expert_out: bfloat16 [4, 4, 4, 80, 2048], P(('groups', 'context'), 'expert', None, None, 'tensor'), parts along dimension 0, may hold values from -6 to 6
- routes: int32 [2048, 2], P(('groups', 'context', 'expert')), parts along dimension 0, may hold values from 0 to 3, all different within a row; in each aligned block of 128 rows (0 to 127, 128 to 255, ...) at most 80 rows name the same one
- route_weights: float32 [2048, 2], P(('groups', 'context', 'expert')), parts along dimension 0, may hold values from 0.1 to 1
- pattern: int32 [8, 8], P(('context', 'expert')), may hold values from 0 to 1, as said below
- lengths: int32 [128], P('groups'), parts along dimension 0, may hold values from 1 to 256, 1024 in all
- teacher: float32 [128, 64], P('groups'), parts along dimension 0, may hold values from 0 to 1
- gain: float32 [2048], P('tensor'), may hold values from 0.5 to 1.5
- head_weight: float32 [2048, 64], P('tensor'), may hold values from -0.125 to 0.125
Outputs:
- grad_query: bfloat16 [2048, 2048], P(('groups', 'context', 'expert'), 'tensor'), parts along dimension 0
- grad_key: float32 [2048, 512], P(('groups', 'context', 'expert'), 'tensor'), parts along dimension 0
- value_gradient: float32 [2048, 512], P(('groups', 'context', 'expert'), 'tensor'), parts along dimension 0
- grad_expert: bfloat16 [4, 4, 4, 80, 2048], P(('groups', 'context'), 'expert', None, None, 'tensor'), parts along dimension 0
The draws below stay inside these ranges and needn't reach their ends.
There are 2 independent parts, one for each index of `groups`. The reference program is written for one: setup_inputs(seed, part) draws one part's arguments, and reference() takes and returns one part's arrays. A program takes and returns all parts, laid end to end along the dimension named above; an argument that names none is the same for every part. Nothing has to cross between parts.
Inputs may be any that keep to these rules, and one draw needn't show every extreme that they name: `pattern`: entry (i, i) is 1; entry (i, j) for i != j is 0 unless i XOR j is a power of two. `routes`: each row names 2 different experts; at most 80 of the pairs of the rows of one device name one expert.
All inputs are finite; a program needn't handle non-finite values.
Results may differ from the reference program's by a relative error of at most 0.0058.
Values may be sent and summed in bfloat16 or wider, within the bound.
A program may use at most 64 MiB of HBM per device.

```python
import math
import jax
import jax.numpy as jnp
import numpy as np
from jax import lax

TOK_DEV = 128
BLOCK_POSITIONS = 128
HEAD_FEATURES = 128
HEADS = 16
KEY_VALUE_HEADS = 4
CATS = 64
TOP = 2
TURNS = 64
LOSS_SCALE = 256
D = 2048
EXPERTS = 4
TOKENS = 1024
NBLK = 8
CAP = 80
N_CONTEXT = 2
N_EXPERT = 4


def query_key_pair(key):
    key_seed = jax.random.fold_in(key, 101)
    query_seed = jax.random.fold_in(key, 202)
    key_vals = jnp.clip(jax.random.normal(key_seed, (TOKENS, KEY_VALUE_HEADS * HEAD_FEATURES), jnp.float32), -5.0, 5.0)
    query_vals = jnp.clip(jax.random.normal(query_seed, (TOKENS, HEADS * HEAD_FEATURES), jnp.float32), -5.0, 5.0)
    return (query_vals, key_vals)


def draw_queries(key, part):
    return query_key_pair(key)[0].astype(jnp.bfloat16)


def draw_keys(key, part):
    return query_key_pair(key)[1].astype(jnp.bfloat16)


def draw_resid(key, part):
    base_seed = jax.random.fold_in(key, 1)
    row_seed = jax.random.fold_in(key, 2)
    col_seed = jax.random.fold_in(key, 3)
    position = jnp.arange(D, dtype=jnp.float32)[None, :] / D
    row_scale = jnp.exp(jax.random.uniform(row_seed, (TOKENS, 1), jnp.float32, math.log(0.2), math.log(2.0)))
    col_scale = jnp.exp(jax.random.uniform(col_seed, (1, D), jnp.float32, math.log(0.3), math.log(3.0)))
    base_draw = jnp.clip(jax.random.normal(base_seed, (TOKENS, D), jnp.float32), -4.0, 4.0)
    col_ramp = jnp.exp(math.log(3.0) * position)
    return (base_draw * row_scale * col_scale * col_ramp).astype(jnp.bfloat16)


def draw_pattern(key, part):
    row_ids = jnp.arange(NBLK, dtype=jnp.int32)[:, None]
    col_ids = jnp.arange(NBLK, dtype=jnp.int32)[None, :]
    differ = jnp.bitwise_xor(row_ids, col_ids)
    single = (differ > 0) & (jnp.bitwise_and(differ, differ - 1) == 0)
    coins = jax.random.randint(key, (NBLK, NBLK), 0, 4) > 0
    return jnp.where(row_ids == col_ids, 1, jnp.where(single & coins, 1, 0)).astype(jnp.int32)


def level_of(stream_key, dims, pieces, least, high):
    def one(dim, blocks):
        steps = jax.random.uniform(jax.random.fold_in(jax.random.fold_in(stream_key, 6), dim), (blocks,), jnp.float32, least / len(pieces), high / len(pieces))
        return jnp.repeat(jnp.exp(steps), dims[dim] // blocks).reshape((-1,) + (1,) * (len(dims) - dim - 1))

    level = one(*pieces[0])
    for cut in pieces[1:]:
        level = level * one(*cut)
    return level


def length_profile(count, total, limit, slope):
    loads = [(1 << 20) // math.isqrt(grade ** slope) + 1 for grade in range(2, count + 1)]
    surplus, counts = total - limit - (count - 1), [1] * (count - 1)
    while surplus > 0:
        movable = [i for i in range(count - 1) if counts[i] < limit]
        pool, left = sum([loads[i] for i in movable]), surplus
        for i in movable:
            more = min(limit - counts[i], max(1, left * loads[i] // pool), surplus)
            counts[i] = counts[i] + more
            surplus = surplus - more
    return np.array([limit] + counts)


def uneven_parts(stream_key, count, total, most, slope):
    if count == 2:
        one = jax.random.randint(stream_key, (), max(1, total - most), min(most, total - 1) + 1)
        return jnp.stack([one, total - one])
    sizes = jnp.asarray(length_profile(count, total, most, slope), jnp.int32)
    twos = (count - 1) // 2
    donor, receiver = sizes[1:1 + 2 * twos:2], sizes[2:2 + 2 * twos:2]
    slack = jnp.minimum(donor - 1, most - receiver)
    passed = jax.random.randint(jax.random.fold_in(stream_key, 1), (twos,), 0, 1 << 20) % (slack + 1)
    sizes = sizes.at[1:1 + 2 * twos:2].set(donor - passed).at[2:2 + 2 * twos:2].set(receiver + passed)
    return sizes[jax.random.permutation(jax.random.fold_in(stream_key, 2), count)]


def routed_block(stream_key, own, number, rows, number_of, top, most, skew):
    sequence = jax.random.permutation(stream_key, number_of)
    packed, ordinary = load_shares(number_of, rows * top, most, skew, True), load_shares(number_of, rows * top, most, skew, False)
    places = jnp.arange(number_of)

    def named(sizes, rotation):
        used = int((sizes > 0).sum())
        fixed = max(1, used // 4)
        moved = fixed + (places - fixed + rotation * (used - fixed)) % max(1, number_of - fixed)
        return jnp.zeros((number_of,), jnp.int32).at[sequence[jnp.where(places < fixed, places, moved)]].set(jnp.asarray(sizes, jnp.int32))

    sizes = jnp.where(number % 4 == 0, named(packed, number // 4), named(ordinary, number - number // 4 - 1))
    mixed = jax.random.permutation(jax.random.fold_in(own, 3), number_of)
    giver, taker = mixed[0:number_of // 2 * 2:2], mixed[1:number_of // 2 * 2:2]
    room = jnp.minimum(sizes[giver] - 1, most - sizes[taker]) // 2
    room = jnp.where((giver == sequence[0]) | (taker == sequence[0]) | (sizes[taker] == 0), 0, jnp.maximum(room, 0))
    moved = jax.random.randint(jax.random.fold_in(own, 4), (number_of // 2,), 0, 1 << 20) % (room + 1)
    sizes = sizes.at[giver].add(-moved).at[taker].add(moved)
    members = jnp.searchsorted(jnp.cumsum(sizes), jnp.arange(rows * top), side="right").astype(jnp.int32)
    grid = members.reshape(top, rows).T
    grid = grid[jax.random.permutation(jax.random.fold_in(own, 1), rows)]
    rotation = jax.random.randint(jax.random.fold_in(own, 2), (rows, 1), 0, top)
    return jnp.take_along_axis(grid, (jnp.arange(top)[None, :] + rotation) % top, axis=1)


def load_shares(number_of, total, limit, skew, full):
    loads = [(1 << 20) // math.isqrt(standing ** skew) + 1 for standing in range(1, number_of + 1)]
    largest = limit if full else min(limit, max(-(-total // number_of), total * loads[0] // sum(loads)))
    least = 1 if total - largest >= number_of - 1 else 0
    given, spare = [largest] + [least] * (number_of - 1), total - largest - least * (number_of - 1)
    while spare > 0:
        movable = [i for i in range(1, number_of) if given[i] < largest] or [i for i in range(1, number_of) if given[i] < limit]
        whole, left = sum([loads[i] for i in movable]), spare
        for i in movable:
            addition = min(limit - given[i], max(1, left * loads[i] // whole), spare)
            given[i] = given[i] + addition
            spare = spare - addition
    return np.array(given)


def noise(key, extent, scale, bound, split=(), kind=jnp.bfloat16):
    array = scale * jax.random.normal(key, extent, jnp.float32)
    if split:
        array = array * level_of(key, extent, split, -0.22, 0.18)
    return jnp.clip(array, -bound, bound).astype(kind)


def setup_inputs(seed: int = 0, part: int = 0) -> dict:
    key_list = jax.random.split(jax.random.key(seed), 13)
    own_keys = jax.random.split(jax.random.fold_in(key_list[12], part), 13)
    queries = draw_queries(jax.random.fold_in(jax.random.fold_in(key_list[12], part), 71), part)
    keys = draw_keys(jax.random.fold_in(jax.random.fold_in(key_list[12], part), 71), part)
    values = noise(own_keys[2], (TOKENS, KEY_VALUE_HEADS * HEAD_FEATURES), 1.0, 6.0, ((0, 8), (1, 2)))
    resid = draw_resid(jax.random.fold_in(jax.random.fold_in(key_list[12], part), 71), part)
    expert_out = noise(own_keys[4], (N_CONTEXT, EXPERTS, N_EXPERT, CAP, D), 1.0, 6.0, ((0, 2), (1, 4), (4, 2)))
    routes_keys = jax.random.split(jax.random.fold_in(own_keys[5], 1), TOKENS // TOK_DEV)
    routes_turns = jax.random.permutation(jax.random.fold_in(own_keys[5], 3), TOKENS // TOK_DEV)
    routes = jax.vmap(lambda own, number: routed_block(jax.random.fold_in(own_keys[5], 2), own, number, TOK_DEV, EXPERTS, TOP, CAP, 2))(routes_keys, routes_turns).reshape((TOKENS, TOP))
    route_weights = jnp.clip(0.1 + 0.9 * jax.random.uniform(own_keys[6], (TOKENS, TOP), jnp.float32) ** level_of(own_keys[6], (TOKENS, TOP), ((0, 8),), -0.2, 0.2), 0.1, 1.0)
    pattern = draw_pattern(jax.random.fold_in(key_list[12], 71), part)
    lengths = uneven_parts(own_keys[8], TURNS, TOKENS, TOKENS // 4, 1).astype(jnp.int32)
    teacher = jnp.clip(jax.random.uniform(own_keys[9], (TURNS, CATS), jnp.float32, 0.0, 1.0), 0.0, 1.0)
    gain = jnp.clip(1.0 + 0.1 * jax.random.normal(key_list[10], (D,), jnp.float32), 0.5, 1.5)
    head_weight = noise(key_list[11], (D, CATS), D ** -0.5, 0.125, ((0, 2),), jnp.float32)
    return {"queries": queries, "keys": keys, "values": values, "resid": resid, "expert_out": expert_out, "routes": routes, "route_weights": route_weights, "pattern": pattern, "lengths": lengths, "teacher": teacher, "gain": gain, "head_weight": head_weight}


EPSILON = 1e-05
NEGATIVE = -1e+30
HIGHEST_PRECISION = lax.Precision.HIGHEST

def turn_index(lengths):
    turn_ends = jnp.cumsum(lengths)
    position = jnp.arange(TOKENS, dtype=jnp.int32)
    return lax.optimization_barrier(jnp.sum((turn_ends[None, :] <= position[:, None]).astype(jnp.int32), axis=1))

def slot_table(routes):
    shard_count = TOKENS // TOK_DEV
    flat_routes = routes.reshape(shard_count, TOK_DEV * TOP)
    onehot = (flat_routes[:, :, None] == jnp.arange(EXPERTS, dtype=jnp.int32)[None, None, :]).astype(jnp.int32)
    rank_table = jnp.cumsum(onehot, axis=1) - onehot
    return lax.optimization_barrier(jnp.sum(rank_table * onehot, axis=2)).reshape(TOKENS, TOP)

def block_starts(block):
    levels = NBLK.bit_length() - 1
    return [block] + [jnp.bitwise_xor(block, jnp.int32(1 << level)) for level in range(levels)]

def block_rows(source, starts):
    return jnp.concatenate([lax.dynamic_slice_in_dim(source, (start * BLOCK_POSITIONS).astype(jnp.int32), BLOCK_POSITIONS, 0) for start in starts], axis=0)

def block_probs(block, queries, keys, pattern):
    starts = block_starts(block)
    group_size = HEADS // KEY_VALUE_HEADS
    query_rows = lax.dynamic_slice_in_dim(queries, (block * BLOCK_POSITIONS).astype(jnp.int32), BLOCK_POSITIONS, 0)
    query_f = query_rows.astype(jnp.float32).reshape(BLOCK_POSITIONS, KEY_VALUE_HEADS, group_size, HEAD_FEATURES)
    key_f = block_rows(keys, starts).astype(jnp.float32).reshape(-1, KEY_VALUE_HEADS, HEAD_FEATURES)
    flag_bits = jnp.stack([jnp.int32(1)] + [pattern[block, start] for start in starts[1:]])
    key_keep = jnp.repeat(flag_bits, BLOCK_POSITIONS) > 0
    scores = jnp.einsum('qkgd,skd->kgqs', query_f, key_f) * HEAD_FEATURES ** (-0.5)
    scores = jnp.where(key_keep[None, None, None, :], scores, NEGATIVE)
    row_max = lax.optimization_barrier(jnp.max(scores, axis=-1, keepdims=True))
    raised = jnp.exp(scores - row_max)
    return (starts, query_f, key_f, raised / lax.optimization_barrier(jnp.sum(raised, axis=-1, keepdims=True)))

def forward_block(block, queries, keys, values, pattern):
    starts, query_f, key_f, attn_prob = block_probs(block, queries, keys, pattern)
    weight_rows = lax.optimization_barrier(attn_prob.astype(jnp.bfloat16)).astype(jnp.float32)
    value_f = block_rows(values, starts).astype(jnp.float32).reshape(-1, KEY_VALUE_HEADS, HEAD_FEATURES)
    return jnp.einsum('kgqs,skd->qkgd', weight_rows, value_f).reshape(BLOCK_POSITIONS, D)

def backward_step(carry, block, queries, keys, values, pattern, grad_out):
    grad_key, value_gradient = carry
    group_size = HEADS // KEY_VALUE_HEADS
    starts, query_f, key_f, attn_prob = block_probs(block, queries, keys, pattern)
    weight_rows = lax.optimization_barrier(attn_prob.astype(jnp.bfloat16)).astype(jnp.float32)
    value_f = block_rows(values, starts).astype(jnp.float32).reshape(-1, KEY_VALUE_HEADS, HEAD_FEATURES)
    out_rows = lax.dynamic_slice_in_dim(grad_out, (block * BLOCK_POSITIONS).astype(jnp.int32), BLOCK_POSITIONS, 0)
    output_float = out_rows.astype(jnp.float32).reshape(BLOCK_POSITIONS, KEY_VALUE_HEADS, group_size, HEAD_FEATURES)
    grad_prob = jnp.einsum('qkgd,skd->kgqs', output_float, value_f)
    value_set_gradient = jnp.einsum('rcnw,nrco->wro', weight_rows, output_float).reshape(-1, KEY_VALUE_HEADS * HEAD_FEATURES)
    row_delta = lax.optimization_barrier(jnp.sum(attn_prob * grad_prob, axis=-1, keepdims=True))
    grad_score = attn_prob * (grad_prob - row_delta) * HEAD_FEATURES ** (-0.5)
    grad_score = lax.optimization_barrier(grad_score.astype(jnp.bfloat16)).astype(jnp.float32)
    grad_query = jnp.einsum('kgqs,skd->qkgd', grad_score, key_f).reshape(BLOCK_POSITIONS, D).astype(jnp.bfloat16)
    grad_kset = jnp.einsum('rcnw,nrco->wro', grad_score, query_f).reshape(-1, KEY_VALUE_HEADS * HEAD_FEATURES)
    for level_count, start in enumerate(starts):
        leading_row = (start * BLOCK_POSITIONS).astype(jnp.int32)
        piece_key = lax.dynamic_slice_in_dim(grad_key, leading_row, BLOCK_POSITIONS, 0) + grad_kset[level_count * BLOCK_POSITIONS:(level_count + 1) * BLOCK_POSITIONS]
        grad_key = lax.dynamic_update_slice_in_dim(grad_key, piece_key, leading_row, 0)
        value_piece = lax.dynamic_slice_in_dim(value_gradient, leading_row, BLOCK_POSITIONS, 0) + value_set_gradient[level_count * BLOCK_POSITIONS:(level_count + 1) * BLOCK_POSITIONS]
        value_gradient = lax.dynamic_update_slice_in_dim(value_gradient, value_piece, leading_row, 0)
    return ((grad_key, value_gradient), grad_query)

def reference(queries, keys, values, resid, expert_out, routes, route_weights, pattern, lengths, teacher, gain, head_weight):
    block_ids = jnp.arange(NBLK, dtype=jnp.int32)
    attention = lax.map(lambda block: forward_block(block, queries, keys, values, pattern), block_ids).reshape(TOKENS, D)
    slot_rank = slot_table(routes)
    shard_id = jnp.arange(TOKENS, dtype=jnp.int32) // TOK_DEV
    context_of = shard_id // N_EXPERT
    source_of = shard_id % N_EXPERT
    mixture = jnp.zeros((TOKENS, D), jnp.float32)
    for choice_k in range(TOP):
        picked = expert_out[context_of, routes[:, choice_k], source_of, slot_rank[:, choice_k]]
        mixture = mixture + route_weights[:, choice_k:choice_k + 1] * picked.astype(jnp.float32)
    hidden = resid.astype(jnp.float32) + attention + mixture
    square_sum = lax.optimization_barrier(jnp.sum(hidden * hidden, axis=1))
    row_rms = jnp.sqrt(square_sum / D + EPSILON)
    normed = hidden / row_rms[:, None] * gain
    logits = jnp.dot(normed, head_weight, precision=HIGHEST_PRECISION)
    target = teacher[turn_index(lengths)]
    grad_logit = (jax.nn.sigmoid(logits) - target) * LOSS_SCALE
    grad_normed = jnp.dot(grad_logit, head_weight.T, precision=HIGHEST_PRECISION)
    inner_sum = lax.optimization_barrier(jnp.sum(grad_normed * gain * hidden, axis=1))
    grad_hidden = gain * grad_normed / row_rms[:, None] - hidden * (inner_sum / (D * row_rms ** 3))[:, None]
    grad_out = grad_hidden.astype(jnp.bfloat16)
    zero_rows = jnp.zeros((TOKENS, KEY_VALUE_HEADS * HEAD_FEATURES), jnp.float32)
    sums, query_blocks = lax.scan(lambda carry, block: backward_step(carry, block, queries, keys, values, pattern, grad_out), (zero_rows, zero_rows), block_ids)
    grad_query = query_blocks.reshape(TOKENS, D)
    grad_expert = jnp.zeros(expert_out.shape, jnp.bfloat16)
    for choice_k in range(TOP):
        scaled = (route_weights[:, choice_k:choice_k + 1] * grad_hidden).astype(jnp.bfloat16)
        grad_expert = grad_expert.at[context_of, routes[:, choice_k], source_of, slot_rank[:, choice_k]].set(scaled)
    return (grad_query, sums[0], sums[1], grad_expert)
```

```python
import functools

import jax
import jax.numpy as jnp
from jax import lax
from jax.experimental import pallas as pl
from jax.experimental.pallas import tpu as pltpu
from jax.sharding import PartitionSpec as P

BLOCK = 128
HEAD = 128
LOSS_SCALE = 256
D = 2048
EPSILON = 1e-05
NEGATIVE = -1e30
LOG2E = 1.4426950408889634
MESH = pl.DeviceIdType.MESH
NT = (((1,), (1,)), ((), ()))
NN = (((1,), (0,)), ((), ()))
TN = (((0,), (0,)), ((), ()))


def dot(a, b, dims):
    return lax.dot_general(a, b, dims, preferred_element_type=jnp.float32)


def flipped(index, bit):
    step = 1 << bit
    return index + step * (1 - 2 * ((index // step) % 2))


def body(
    n_context,
    n_expert,
    q_hbm,
    k_hbm,
    v_hbm,
    r_hbm,
    x_hbm,
    routes_hbm,
    rw_hbm,
    pat_hbm,
    len_hbm,
    tea_hbm,
    gain_hbm,
    hw_hbm,
    gq_v,
    gk_v,
    gv_v,
    gx_hbm,
    q_v,
    r_v,
    kbuf,
    vbuf,
    xbuf,
    routes_v,
    rw_v,
    pat_s,
    len_v,
    tea_v,
    gain_v,
    hw_v,
    qst,
    pt_v,
    ptb_v,
    attn_v,
    hid_v,
    dost,
    hw3_v,
    ex_send,
    ex_recv,
    gsend,
    grecv,
    xsend,
    in_sem,
    kv_send_sem,
    kv_recv_sem,
    x_send_sem,
    x_recv_sem,
    ex_sem,
    g_send_sem,
    g_recv_sem,
    gx_send_sem,
    gx_recv_sem,
):
    ctx = lax.axis_index("context")
    exp = lax.axis_index("expert")
    ten = lax.axis_index("tensor")
    shard = ctx * n_expert + exp
    e_bits = n_expert.bit_length() - 1
    c_bits = n_context.bit_length() - 1
    bits = e_bits + c_bits
    rows = q_v.shape[0]
    width = q_v.shape[1]
    kv_dev = kbuf.shape[2] // HEAD
    group = width // HEAD // kv_dev
    cap = xbuf.shape[1]
    span = (1 + bits) * BLOCK
    cats = hw_v.shape[0]
    turns = tea_v.shape[0]
    scale = HEAD ** (-0.5)

    def partner(bit):
        if bit < e_bits:
            return {"expert": flipped(exp, bit)}
        return {"context": flipped(ctx, bit - e_bits)}

    others = [{"expert": lax.rem(exp + off, n_expert)} for off in range(1, n_expert)]
    peers = others + [partner(bit) for bit in range(e_bits, bits)] + [{"tensor": 1 - ten}]
    barrier = pltpu.get_barrier_semaphore()
    for peer in peers:
        pl.semaphore_signal(barrier, inc=1, device_id=peer, device_id_type=MESH)

    local_list = [
        (q_hbm, q_v),
        (k_hbm, kbuf.at[0]),
        (v_hbm, vbuf.at[0]),
        (r_hbm, r_v),
        (x_hbm.at[0, 0, exp], xbuf.at[exp]),
        (routes_hbm, routes_v),
        (rw_hbm, rw_v),
        (pat_hbm, pat_s),
        (len_hbm, len_v),
        (tea_hbm, tea_v),
        (gain_hbm, gain_v),
        (hw_hbm, hw_v),
    ]
    local = [
        pltpu.make_async_copy(src, dst, in_sem.at[i]) for i, (src, dst) in enumerate(local_list)
    ]
    for copy in local:
        copy.start()
    pl.semaphore_wait(barrier, len(peers))

    kv_copies = []
    for bit in range(bits):
        for j, (src, dst) in enumerate(((k_hbm, kbuf), (v_hbm, vbuf))):
            copy = pltpu.make_async_remote_copy(
                src_ref=src,
                dst_ref=dst.at[1 + bit],
                send_sem=kv_send_sem.at[2 * bit + j],
                recv_sem=kv_recv_sem.at[2 * bit + j],
                device_id=partner(bit),
                device_id_type=MESH,
            )
            copy.start()
            kv_copies.append(copy)
    x_copies = []
    for off in range(1, n_expert):
        copy = pltpu.make_async_remote_copy(
            src_ref=x_hbm.at[0, 0, lax.rem(exp + off, n_expert)],
            dst_ref=xbuf.at[exp],
            send_sem=x_send_sem.at[off],
            recv_sem=x_recv_sem.at[off],
            device_id=others[off - 1],
            device_id_type=MESH,
        )
        copy.start()
        x_copies.append(copy)
    for copy in local:
        copy.wait()

    lane = lax.broadcasted_iota(jnp.int32, (rows, 128), 1)
    name = lax.broadcasted_iota(jnp.int32, (128, rows), 0)
    row = lax.broadcasted_iota(jnp.int32, (rows, rows), 0)
    col = lax.broadcasted_iota(jnp.int32, (rows, rows), 1)
    member = jnp.zeros((128, rows), jnp.float32)
    weight = jnp.zeros((128, rows), jnp.float32)
    for k in range(routes_v.shape[0]):
        hit = routes_v[k : k + 1, :] == name
        member = member + jnp.where(hit, 1.0, 0.0)
        weight = weight + jnp.where(hit, rw_v[k : k + 1, :], 0.0)
    before = dot(
        member.astype(jnp.bfloat16), jnp.where(row < col, 1.0, 0.0).astype(jnp.bfloat16), NN
    )
    slot = jnp.where(member > 0, before, -1.0).T
    weight = weight.T
    cap_lane = lax.broadcasted_iota(jnp.int32, (rows, cap), 1).astype(jnp.float32)

    def expert_pick(index):
        mine = lane == index
        slot_col = jnp.sum(jnp.where(mine, slot, 0.0), axis=1, keepdims=True)
        weight_col = jnp.sum(jnp.where(mine, weight, 0.0), axis=1, keepdims=True)
        onehot = jnp.where(slot_col == cap_lane, 1.0, 0.0).astype(jnp.bfloat16)
        return onehot, weight_col

    turn_row = lax.broadcasted_iota(jnp.int32, (turns, turns), 0)
    turn_col = lax.broadcasted_iota(jnp.int32, (turns, turns), 1)
    length_row = len_v[...].astype(jnp.float32)
    ends = jnp.sum(jnp.where(turn_col <= turn_row, length_row, 0.0), axis=1, keepdims=True)
    starts = jnp.sum(jnp.where(turn_col < turn_row, length_row, 0.0), axis=1, keepdims=True)
    position = (
        lax.broadcasted_iota(jnp.int32, (turns, rows), 1) + shard * rows
    ).astype(jnp.float32)
    turn_pick = jnp.where((starts <= position) & (position < ends), 1.0, 0.0)
    target = lax.dot_general(
        turn_pick,
        tea_v[...],
        TN,
        precision=lax.Precision.HIGHEST,
        preferred_element_type=jnp.float32,
    )

    hw = hw_v[...]
    hw_hi = hw.astype(jnp.bfloat16)
    hw_lo = (hw - hw_hi.astype(jnp.float32)).astype(jnp.bfloat16)
    hw3_v[...] = jnp.concatenate([hw_hi, hw_lo, hw_hi], axis=0)

    for g in range(kv_dev):
        for h in range(group):
            head = g * group + h
            qst[g, h * rows : (h + 1) * rows, :] = q_v[:, head * HEAD : (head + 1) * HEAD]

    for copy in kv_copies:
        copy.wait_recv()
    keep = [jnp.float32(1.0)]
    for bit in range(bits):
        other = flipped(exp, bit) + ctx * n_expert
        if bit >= e_bits:
            other = flipped(ctx, bit - e_bits) * n_expert + exp
        keep.append(pat_s[0, other].astype(jnp.float32))
    for g in range(kv_dev):
        lanes = slice(g * HEAD, (g + 1) * HEAD)
        parts = []
        for b in range(1 + bits):
            s = dot(kbuf[b, :, lanes], qst[g], NT)
            if b == 0:
                parts.append(s * (scale * LOG2E))
            else:
                parts.append(s * (keep[b] * (scale * LOG2E)) + (1.0 - keep[b]) * NEGATIVE)
        top_score = functools.reduce(
            jnp.maximum, [jnp.max(s, axis=0, keepdims=True) for s in parts]
        )
        parts = [jnp.exp2(s - top_score) for s in parts]
        total = functools.reduce(jnp.add, [jnp.sum(s, axis=0, keepdims=True) for s in parts])
        inverse = 1.0 / total
        for b in range(1 + bits):
            prob = parts[b] * inverse
            pt_v[g, b * BLOCK : (b + 1) * BLOCK, :] = prob
            ptb_v[g, b * BLOCK : (b + 1) * BLOCK, :] = prob.astype(jnp.bfloat16)
        value_set = vbuf[:, :, lanes].reshape(span, HEAD)
        out_t = dot(value_set, ptb_v[g], TN)
        for h in range(group):
            head = g * group + h
            attn_v[:, head * HEAD : (head + 1) * HEAD] = out_t[:, h * rows : (h + 1) * rows].T

    hid_v[...] = r_v[...].astype(jnp.float32) + attn_v[...]
    for off in range(n_expert):
        source = lax.rem(exp - off + n_expert, n_expert)
        if off:
            pltpu.make_async_copy(xbuf.at[source], xbuf.at[source], x_recv_sem.at[off]).wait()
        onehot, weight_col = expert_pick(source)
        hid_v[...] += weight_col * dot(onehot, xbuf[source], NN)

    hidden = hid_v[...]
    gain = gain_v[...]
    square = jnp.sum(hidden * hidden, axis=1, keepdims=True)
    scaled = hidden * gain
    part_hi = scaled.astype(jnp.bfloat16)
    part_lo = (scaled - part_hi.astype(jnp.float32)).astype(jnp.bfloat16)
    first = dot(part_hi, hw3_v[: 2 * cats, :], NT)
    raw_part = first[:, :cats] + first[:, cats:] + dot(part_lo, hw3_v[:cats, :], NT)
    ex_send[...] = jnp.concatenate([raw_part, jnp.broadcast_to(square, (rows, 128 - cats))], axis=1)
    ex_copy = pltpu.make_async_remote_copy(
        src_ref=ex_send,
        dst_ref=ex_recv,
        send_sem=ex_sem.at[0],
        recv_sem=ex_sem.at[1],
        device_id={"tensor": 1 - ten},
        device_id_type=MESH,
    )
    ex_copy.start()
    ex_copy.wait()
    both = ex_send[...] + ex_recv[...]
    raw = both[:, :cats]
    rms = jnp.sqrt(both[:, cats : cats + 1] / D + EPSILON)
    inv = 1.0 / rms
    grad_logit = (jax.nn.sigmoid(raw * inv) - target) * LOSS_SCALE
    inner = jnp.sum(grad_logit * raw, axis=1, keepdims=True)
    gl_hi = grad_logit.astype(jnp.bfloat16)
    gl_lo = (grad_logit - gl_hi.astype(jnp.float32)).astype(jnp.bfloat16)
    normed = dot(jnp.concatenate([gl_hi, gl_hi, gl_lo], axis=1), hw3_v[...], NN)
    grad_hidden = gain * normed * inv - hidden * (inner / (D * rms * rms * rms))
    hid_v[...] = grad_hidden

    gx_copies = []
    for off in list(range(1, n_expert)) + [0]:
        owner = lax.rem(exp + off, n_expert)
        onehot, weight_col = expert_pick(owner)
        weighted = (weight_col * hid_v[...]).astype(jnp.bfloat16)
        xsend[off] = dot(onehot, weighted, TN).astype(jnp.bfloat16)
        if off:
            copy = pltpu.make_async_remote_copy(
                src_ref=xsend.at[off],
                dst_ref=gx_hbm.at[0, 0, exp],
                send_sem=gx_send_sem.at[off],
                recv_sem=gx_recv_sem.at[off],
                device_id=others[off - 1],
                device_id_type=MESH,
            )
        else:
            copy = pltpu.make_async_copy(xsend.at[0], gx_hbm.at[0, 0, exp], gx_send_sem.at[0])
        copy.start()
        gx_copies.append(copy)

    for g in range(kv_dev):
        for h in range(group):
            head = g * group + h
            dost[g, h * rows : (h + 1) * rows, :] = hid_v[
                :, head * HEAD : (head + 1) * HEAD
            ].astype(jnp.bfloat16)
    for g in range(kv_dev):
        lanes = slice(g * HEAD, (g + 1) * HEAD)
        key_set = kbuf[:, :, lanes].reshape(span, HEAD)
        value_set = vbuf[:, :, lanes].reshape(span, HEAD)
        grad_prob = dot(value_set, dost[g], NT)
        prob = pt_v[g]
        delta = jnp.sum(prob * grad_prob, axis=0, keepdims=True)
        score = (prob * (grad_prob - delta) * scale).astype(jnp.bfloat16)
        key_grad = dot(score, qst[g], NN)
        value_grad = dot(ptb_v[g], dost[g], NN)
        gk_v[:, lanes] = key_grad[:BLOCK]
        gv_v[:, lanes] = value_grad[:BLOCK]
        for b in range(bits):
            rows_b = slice((1 + b) * BLOCK, (2 + b) * BLOCK)
            gsend[b, 0, :, lanes] = key_grad[rows_b].astype(jnp.bfloat16)
            gsend[b, 1, :, lanes] = value_grad[rows_b].astype(jnp.bfloat16)
        query_t = dot(key_set, score, TN)
        for h in range(group):
            head = g * group + h
            gq_v[:, head * HEAD : (head + 1) * HEAD] = query_t[:, h * rows : (h + 1) * rows].T.astype(
                jnp.bfloat16
            )
    g_copies = []
    for bit in range(bits):
        copy = pltpu.make_async_remote_copy(
            src_ref=gsend.at[bit],
            dst_ref=grecv.at[bit],
            send_sem=g_send_sem.at[bit],
            recv_sem=g_recv_sem.at[bit],
            device_id=partner(bit),
            device_id_type=MESH,
        )
        copy.start()
        g_copies.append(copy)
    for bit in range(bits):
        g_copies[bit].wait_recv()
        gk_v[...] += grecv[bit, 0].astype(jnp.float32)
        gv_v[...] += grecv[bit, 1].astype(jnp.float32)
    for copy in kv_copies + x_copies + g_copies:
        copy.wait_send()
    for copy in gx_copies:
        copy.wait()


def solution(mesh):
    n_context = mesh.shape["context"]
    n_expert = mesh.shape["expert"]
    bits = (n_context * n_expert).bit_length() - 1

    def local(
        queries,
        keys,
        values,
        resid,
        expert_out,
        routes,
        route_weights,
        pattern,
        lengths,
        teacher,
        gain,
        head_weight,
    ):
        rows, width = queries.shape
        kv_width = keys.shape[1]
        kv_dev = kv_width // HEAD
        group = width // HEAD // kv_dev
        span = (1 + bits) * BLOCK
        cap = expert_out.shape[3]
        lengths = lengths.reshape(1, -1)
        gain = gain.reshape(1, -1)
        cats = head_weight.shape[1]
        head_weight, routes, route_weights = head_weight.T, routes.T, route_weights.T
        bf16, f32 = jnp.bfloat16, jnp.float32
        dma = pltpu.SemaphoreType.DMA
        args = (
            queries,
            keys,
            values,
            resid,
            expert_out,
            routes,
            route_weights,
            pattern,
            lengths,
            teacher,
            gain,
            head_weight,
        )
        scratch = [
            pltpu.VMEM((rows, width), bf16),
            pltpu.VMEM((rows, width), bf16),
            pltpu.VMEM((1 + bits, rows, kv_width), bf16),
            pltpu.VMEM((1 + bits, rows, kv_width), bf16),
            pltpu.VMEM((n_expert, cap, width), bf16),
            pltpu.VMEM(routes.shape, jnp.int32),
            pltpu.VMEM(route_weights.shape, f32),
            pltpu.SMEM(pattern.shape, jnp.int32),
            pltpu.VMEM(lengths.shape, jnp.int32),
            pltpu.VMEM(teacher.shape, f32),
            pltpu.VMEM(gain.shape, f32),
            pltpu.VMEM(head_weight.shape, f32),
            pltpu.VMEM((kv_dev, group * rows, HEAD), bf16),
            pltpu.VMEM((kv_dev, span, group * rows), f32),
            pltpu.VMEM((kv_dev, span, group * rows), bf16),
            pltpu.VMEM((rows, width), f32),
            pltpu.VMEM((rows, width), f32),
            pltpu.VMEM((kv_dev, group * rows, HEAD), bf16),
            pltpu.VMEM((3 * cats, width), bf16),
            pltpu.VMEM((rows, 128), f32),
            pltpu.VMEM((rows, 128), f32),
            pltpu.VMEM((bits, 2, rows, kv_width), bf16),
            pltpu.VMEM((bits, 2, rows, kv_width), bf16),
            pltpu.VMEM((n_expert, cap, width), bf16),
            dma((len(args),)),
            dma((2 * bits,)),
            dma((2 * bits,)),
            dma((n_expert,)),
            dma((n_expert,)),
            dma((2,)),
            dma((bits,)),
            dma((bits,)),
            dma((n_expert,)),
            dma((n_expert,)),
        ]
        return pl.pallas_call(
            functools.partial(body, n_context, n_expert),
            out_shape=(
                jax.ShapeDtypeStruct((rows, width), bf16),
                jax.ShapeDtypeStruct((rows, kv_width), f32),
                jax.ShapeDtypeStruct((rows, kv_width), f32),
                jax.ShapeDtypeStruct(expert_out.shape, bf16),
            ),
            in_specs=[pl.BlockSpec(memory_space=pltpu.HBM)] * len(args),
            out_specs=(pl.BlockSpec(memory_space=pltpu.VMEM),) * 4,
            scratch_shapes=scratch,
            compiler_params=pltpu.CompilerParams(
                collective_id=0, has_side_effects=True, vmem_limit_bytes=48 * 1024 * 1024
            ),
        )(*args)

    rows_spec = P(("groups", "context", "expert"), "tensor")
    expert_spec = P(("groups", "context"), "expert", None, None, "tensor")
    return jax.shard_map(
        local,
        mesh=mesh,
        in_specs=(
            rows_spec,
            rows_spec,
            rows_spec,
            rows_spec,
            expert_spec,
            P(("groups", "context", "expert"), None),
            P(("groups", "context", "expert"), None),
            P(("context", "expert"), None),
            P("groups"),
            P("groups", None),
            P("tensor"),
            P("tensor", None),
        ),
        out_specs=(rows_spec, rows_spec, rows_spec, expert_spec),
        check_vma=False,
    )
```

```python
import functools

import jax
import jax.numpy as jnp
from jax import lax
from jax.experimental import pallas as pl
from jax.experimental.pallas import tpu as pltpu
from jax.sharding import PartitionSpec as P

BLOCK = 128
HEAD = 128
LOSS_SCALE = 256
D = 2048
EPSILON = 1e-05
NEGATIVE = -1e30
LOG2E = 1.4426950408889634
MESH = pl.DeviceIdType.MESH
NT = (((1,), (1,)), ((), ()))
NN = (((1,), (0,)), ((), ()))
TN = (((0,), (0,)), ((), ()))


def dot(a, b, dims):
    return lax.dot_general(a, b, dims, preferred_element_type=jnp.float32)


def flipped(index, bit):
    step = 1 << bit
    return index + step * (1 - 2 * ((index // step) % 2))


def body(
    n_context,
    n_expert,
    q_hbm,
    k_hbm,
    v_hbm,
    r_hbm,
    x_hbm,
    routes_hbm,
    rw_hbm,
    pat_hbm,
    len_hbm,
    tea_hbm,
    gain_hbm,
    hw_hbm,
    gq_hbm,
    gk_hbm,
    gv_hbm,
    gx_hbm,
    q_v,
    r_v,
    kbuf,
    vbuf,
    xbuf,
    routes_v,
    rw_v,
    pat_s,
    len_v,
    tea_v,
    gain_v,
    hw_v,
    qst,
    pt_v,
    ptb_v,
    attn_v,
    hid_v,
    dost,
    hw3_v,
    ex_send,
    ex_recv,
    gsend,
    grecv,
    xsend,
    gq_v,
    gk_v,
    gv_v,
    in_sem,
    kv_send_sem,
    kv_recv_sem,
    x_send_sem,
    x_recv_sem,
    ex_sem,
    g_send_sem,
    g_recv_sem,
    gx_send_sem,
    gx_recv_sem,
    out_sem,
):
    ctx = lax.axis_index("context")
    exp = lax.axis_index("expert")
    ten = lax.axis_index("tensor")
    shard = ctx * n_expert + exp
    e_bits = n_expert.bit_length() - 1
    c_bits = n_context.bit_length() - 1
    bits = e_bits + c_bits
    rows = q_v.shape[0]
    width = q_v.shape[1]
    kv_dev = kbuf.shape[2] // HEAD
    group = width // HEAD // kv_dev
    cap = xbuf.shape[1]
    span = (1 + bits) * BLOCK
    cats = hw_v.shape[0]
    turns = tea_v.shape[0]
    scale = HEAD ** (-0.5)

    def partner(bit):
        if bit < e_bits:
            return {"expert": flipped(exp, bit)}
        return {"context": flipped(ctx, bit - e_bits)}

    others = [{"expert": lax.rem(exp + off, n_expert)} for off in range(1, n_expert)]
    peers = others + [partner(bit) for bit in range(e_bits, bits)] + [{"tensor": 1 - ten}]
    barrier = pltpu.get_barrier_semaphore()
    for peer in peers:
        pl.semaphore_signal(barrier, inc=1, device_id=peer, device_id_type=MESH)

    local_list = [
        (q_hbm, q_v),
        (k_hbm, kbuf.at[0]),
        (v_hbm, vbuf.at[0]),
        (r_hbm, r_v),
        (x_hbm.at[0, 0, exp], xbuf.at[exp]),
        (routes_hbm, routes_v),
        (rw_hbm, rw_v),
        (pat_hbm, pat_s),
        (len_hbm, len_v),
        (tea_hbm, tea_v),
        (gain_hbm, gain_v),
        (hw_hbm, hw_v),
    ]
    local = [
        pltpu.make_async_copy(src, dst, in_sem.at[i]) for i, (src, dst) in enumerate(local_list)
    ]
    for copy in local:
        copy.start()
    pl.semaphore_wait(barrier, len(peers))

    kv_copies = []
    for bit in range(bits):
        for j, (src, dst) in enumerate(((k_hbm, kbuf), (v_hbm, vbuf))):
            copy = pltpu.make_async_remote_copy(
                src_ref=src,
                dst_ref=dst.at[1 + bit],
                send_sem=kv_send_sem.at[2 * bit + j],
                recv_sem=kv_recv_sem.at[2 * bit + j],
                device_id=partner(bit),
                device_id_type=MESH,
            )
            copy.start()
            kv_copies.append(copy)
    x_copies = []
    for off in range(1, n_expert):
        copy = pltpu.make_async_remote_copy(
            src_ref=x_hbm.at[0, 0, lax.rem(exp + off, n_expert)],
            dst_ref=xbuf.at[exp],
            send_sem=x_send_sem.at[off],
            recv_sem=x_recv_sem.at[off],
            device_id=others[off - 1],
            device_id_type=MESH,
        )
        copy.start()
        x_copies.append(copy)
    for copy in local:
        copy.wait()

    lane = lax.broadcasted_iota(jnp.int32, (rows, 128), 1)
    name = lax.broadcasted_iota(jnp.int32, (128, rows), 0)
    row = lax.broadcasted_iota(jnp.int32, (rows, rows), 0)
    col = lax.broadcasted_iota(jnp.int32, (rows, rows), 1)
    member = jnp.zeros((128, rows), jnp.float32)
    weight = jnp.zeros((128, rows), jnp.float32)
    for k in range(routes_v.shape[0]):
        hit = routes_v[k : k + 1, :] == name
        member = member + jnp.where(hit, 1.0, 0.0)
        weight = weight + jnp.where(hit, rw_v[k : k + 1, :], 0.0)
    before = dot(
        member.astype(jnp.bfloat16), jnp.where(row < col, 1.0, 0.0).astype(jnp.bfloat16), NN
    )
    slot = jnp.where(member > 0, before, -1.0).T
    weight = weight.T
    cap_lane = lax.broadcasted_iota(jnp.int32, (rows, cap), 1).astype(jnp.float32)

    def expert_pick(index):
        mine = lane == index
        slot_col = jnp.sum(jnp.where(mine, slot, 0.0), axis=1, keepdims=True)
        weight_col = jnp.sum(jnp.where(mine, weight, 0.0), axis=1, keepdims=True)
        onehot = jnp.where(slot_col == cap_lane, 1.0, 0.0).astype(jnp.bfloat16)
        return onehot, weight_col

    turn_row = lax.broadcasted_iota(jnp.int32, (turns, turns), 0)
    turn_col = lax.broadcasted_iota(jnp.int32, (turns, turns), 1)
    length_row = len_v[...].astype(jnp.float32)
    ends = jnp.sum(jnp.where(turn_col <= turn_row, length_row, 0.0), axis=1, keepdims=True)
    starts = jnp.sum(jnp.where(turn_col < turn_row, length_row, 0.0), axis=1, keepdims=True)
    position = (
        lax.broadcasted_iota(jnp.int32, (turns, rows), 1) + shard * rows
    ).astype(jnp.float32)
    turn_pick = jnp.where((starts <= position) & (position < ends), 1.0, 0.0)
    target = lax.dot_general(
        turn_pick,
        tea_v[...],
        TN,
        precision=lax.Precision.HIGHEST,
        preferred_element_type=jnp.float32,
    )

    hw = hw_v[...]
    hw_hi = hw.astype(jnp.bfloat16)
    hw_lo = (hw - hw_hi.astype(jnp.float32)).astype(jnp.bfloat16)
    hw3_v[...] = jnp.concatenate([hw_hi, hw_lo, hw_hi], axis=0)

    for g in range(kv_dev):
        for h in range(group):
            head = g * group + h
            qst[g, h * rows : (h + 1) * rows, :] = q_v[:, head * HEAD : (head + 1) * HEAD]

    for copy in kv_copies:
        copy.wait_recv()
    keep = [jnp.float32(1.0)]
    for bit in range(bits):
        other = flipped(exp, bit) + ctx * n_expert
        if bit >= e_bits:
            other = flipped(ctx, bit - e_bits) * n_expert + exp
        keep.append(pat_s[0, other].astype(jnp.float32))
    for g in range(kv_dev):
        lanes = slice(g * HEAD, (g + 1) * HEAD)
        parts = []
        for b in range(1 + bits):
            s = dot(kbuf[b, :, lanes], qst[g], NT)
            if b == 0:
                parts.append(s * (scale * LOG2E))
            else:
                parts.append(s * (keep[b] * (scale * LOG2E)) + (1.0 - keep[b]) * NEGATIVE)
        top_score = functools.reduce(
            jnp.maximum, [jnp.max(s, axis=0, keepdims=True) for s in parts]
        )
        parts = [jnp.exp2(s - top_score) for s in parts]
        total = functools.reduce(jnp.add, [jnp.sum(s, axis=0, keepdims=True) for s in parts])
        inverse = 1.0 / total
        for b in range(1 + bits):
            prob = parts[b] * inverse
            pt_v[g, b * BLOCK : (b + 1) * BLOCK, :] = prob
            ptb_v[g, b * BLOCK : (b + 1) * BLOCK, :] = prob.astype(jnp.bfloat16)
        value_set = vbuf[:, :, lanes].reshape(span, HEAD)
        out_t = dot(value_set, ptb_v[g], TN)
        for h in range(group):
            head = g * group + h
            attn_v[:, head * HEAD : (head + 1) * HEAD] = out_t[:, h * rows : (h + 1) * rows].T

    hid_v[...] = r_v[...].astype(jnp.float32) + attn_v[...]
    for off in range(n_expert):
        source = lax.rem(exp - off + n_expert, n_expert)
        if off:
            pltpu.make_async_copy(xbuf.at[source], xbuf.at[source], x_recv_sem.at[off]).wait()
        onehot, weight_col = expert_pick(source)
        hid_v[...] += weight_col * dot(onehot, xbuf[source], NN)

    hidden = hid_v[...]
    gain = gain_v[...]
    square = jnp.sum(hidden * hidden, axis=1, keepdims=True)
    scaled = hidden * gain
    part_hi = scaled.astype(jnp.bfloat16)
    part_lo = (scaled - part_hi.astype(jnp.float32)).astype(jnp.bfloat16)
    first = dot(part_hi, hw3_v[: 2 * cats, :], NT)
    raw_part = first[:, :cats] + first[:, cats:] + dot(part_lo, hw3_v[:cats, :], NT)
    ex_send[...] = jnp.concatenate([raw_part, jnp.broadcast_to(square, (rows, 128 - cats))], axis=1)
    ex_copy = pltpu.make_async_remote_copy(
        src_ref=ex_send,
        dst_ref=ex_recv,
        send_sem=ex_sem.at[0],
        recv_sem=ex_sem.at[1],
        device_id={"tensor": 1 - ten},
        device_id_type=MESH,
    )
    ex_copy.start()
    ex_copy.wait()
    both = ex_send[...] + ex_recv[...]
    raw = both[:, :cats]
    rms = jnp.sqrt(both[:, cats : cats + 1] / D + EPSILON)
    inv = 1.0 / rms
    grad_logit = (jax.nn.sigmoid(raw * inv) - target) * LOSS_SCALE
    inner = jnp.sum(grad_logit * raw, axis=1, keepdims=True)
    gl_hi = grad_logit.astype(jnp.bfloat16)
    gl_lo = (grad_logit - gl_hi.astype(jnp.float32)).astype(jnp.bfloat16)
    normed = dot(jnp.concatenate([gl_hi, gl_hi, gl_lo], axis=1), hw3_v[...], NN)
    grad_hidden = gain * normed * inv - hidden * (inner / (D * rms * rms * rms))
    hid_v[...] = grad_hidden

    gx_copies = []
    for off in list(range(1, n_expert)) + [0]:
        owner = lax.rem(exp + off, n_expert)
        onehot, weight_col = expert_pick(owner)
        weighted = (weight_col * hid_v[...]).astype(jnp.bfloat16)
        xsend[off] = dot(onehot, weighted, TN).astype(jnp.bfloat16)
        if off:
            copy = pltpu.make_async_remote_copy(
                src_ref=xsend.at[off],
                dst_ref=gx_hbm.at[0, 0, exp],
                send_sem=gx_send_sem.at[off],
                recv_sem=gx_recv_sem.at[off],
                device_id=others[off - 1],
                device_id_type=MESH,
            )
        else:
            copy = pltpu.make_async_copy(xsend.at[0], gx_hbm.at[0, 0, exp], gx_send_sem.at[0])
        copy.start()
        gx_copies.append(copy)

    for g in range(kv_dev):
        for h in range(group):
            head = g * group + h
            dost[g, h * rows : (h + 1) * rows, :] = hid_v[
                :, head * HEAD : (head + 1) * HEAD
            ].astype(jnp.bfloat16)
    for g in range(kv_dev):
        lanes = slice(g * HEAD, (g + 1) * HEAD)
        key_set = kbuf[:, :, lanes].reshape(span, HEAD)
        value_set = vbuf[:, :, lanes].reshape(span, HEAD)
        grad_prob = dot(value_set, dost[g], NT)
        prob = pt_v[g]
        delta = jnp.sum(prob * grad_prob, axis=0, keepdims=True)
        score = (prob * (grad_prob - delta) * scale).astype(jnp.bfloat16)
        key_grad = dot(score, qst[g], NN)
        value_grad = dot(ptb_v[g], dost[g], NN)
        gk_v[:, lanes] = key_grad[:BLOCK]
        gv_v[:, lanes] = value_grad[:BLOCK]
        for b in range(bits):
            rows_b = slice((1 + b) * BLOCK, (2 + b) * BLOCK)
            gsend[b, 0, :, lanes] = key_grad[rows_b].astype(jnp.bfloat16)
            gsend[b, 1, :, lanes] = value_grad[rows_b].astype(jnp.bfloat16)
        query_t = dot(key_set, score, TN)
        for h in range(group):
            head = g * group + h
            gq_v[:, head * HEAD : (head + 1) * HEAD] = query_t[:, h * rows : (h + 1) * rows].T.astype(
                jnp.bfloat16
            )
    g_copies = []
    for bit in range(bits):
        copy = pltpu.make_async_remote_copy(
            src_ref=gsend.at[bit],
            dst_ref=grecv.at[bit],
            send_sem=g_send_sem.at[bit],
            recv_sem=g_recv_sem.at[bit],
            device_id=partner(bit),
            device_id_type=MESH,
        )
        copy.start()
        g_copies.append(copy)
    gq_copy = pltpu.make_async_copy(gq_v, gq_hbm, out_sem.at[0])
    gq_copy.start()
    for bit in range(bits):
        g_copies[bit].wait_recv()
        gk_v[...] += grecv[bit, 0].astype(jnp.float32)
        gv_v[...] += grecv[bit, 1].astype(jnp.float32)
    gk_copy = pltpu.make_async_copy(gk_v, gk_hbm, out_sem.at[1])
    gk_copy.start()
    gv_copy = pltpu.make_async_copy(gv_v, gv_hbm, out_sem.at[2])
    gv_copy.start()
    for copy in kv_copies + x_copies + g_copies:
        copy.wait_send()
    for copy in gx_copies:
        copy.wait()
    gq_copy.wait()
    gk_copy.wait()
    gv_copy.wait()


def finish(*refs):
    sources, results, held, sems = refs[:4], refs[4:8], refs[8:12], refs[12]
    pieces = list(zip(sources[:3], results[:3], held[:3]))
    for i in range(held[3].shape[0]):
        pieces.append((sources[3].at[0, 0, i], results[3].at[0, 0, i], held[3].at[i]))
    loads = [
        pltpu.make_async_copy(src, mid, sems.at[0, i]) for i, (src, _, mid) in enumerate(pieces)
    ]
    stores = [
        pltpu.make_async_copy(mid, dst, sems.at[1, i]) for i, (_, dst, mid) in enumerate(pieces)
    ]
    for load in loads:
        load.start()
    for load, store in zip(loads, stores):
        load.wait()
        store.start()
    for store in stores:
        store.wait()


def solution(mesh):
    n_context = mesh.shape["context"]
    n_expert = mesh.shape["expert"]
    bits = (n_context * n_expert).bit_length() - 1

    def local(
        queries,
        keys,
        values,
        resid,
        expert_out,
        routes,
        route_weights,
        pattern,
        lengths,
        teacher,
        gain,
        head_weight,
    ):
        rows, width = queries.shape
        kv_width = keys.shape[1]
        kv_dev = kv_width // HEAD
        group = width // HEAD // kv_dev
        span = (1 + bits) * BLOCK
        cap = expert_out.shape[3]
        lengths = lengths.reshape(1, -1)
        gain = gain.reshape(1, -1)
        cats = head_weight.shape[1]
        head_weight, routes, route_weights = head_weight.T, routes.T, route_weights.T
        bf16, f32 = jnp.bfloat16, jnp.float32
        dma = pltpu.SemaphoreType.DMA
        args = (
            queries,
            keys,
            values,
            resid,
            expert_out,
            routes,
            route_weights,
            pattern,
            lengths,
            teacher,
            gain,
            head_weight,
        )
        scratch = [
            pltpu.VMEM((rows, width), bf16),
            pltpu.VMEM((rows, width), bf16),
            pltpu.VMEM((1 + bits, rows, kv_width), bf16),
            pltpu.VMEM((1 + bits, rows, kv_width), bf16),
            pltpu.VMEM((n_expert, cap, width), bf16),
            pltpu.VMEM(routes.shape, jnp.int32),
            pltpu.VMEM(route_weights.shape, f32),
            pltpu.SMEM(pattern.shape, jnp.int32),
            pltpu.VMEM(lengths.shape, jnp.int32),
            pltpu.VMEM(teacher.shape, f32),
            pltpu.VMEM(gain.shape, f32),
            pltpu.VMEM(head_weight.shape, f32),
            pltpu.VMEM((kv_dev, group * rows, HEAD), bf16),
            pltpu.VMEM((kv_dev, span, group * rows), f32),
            pltpu.VMEM((kv_dev, span, group * rows), bf16),
            pltpu.VMEM((rows, width), f32),
            pltpu.VMEM((rows, width), f32),
            pltpu.VMEM((kv_dev, group * rows, HEAD), bf16),
            pltpu.VMEM((3 * cats, width), bf16),
            pltpu.VMEM((rows, 128), f32),
            pltpu.VMEM((rows, 128), f32),
            pltpu.VMEM((bits, 2, rows, kv_width), bf16),
            pltpu.VMEM((bits, 2, rows, kv_width), bf16),
            pltpu.VMEM((n_expert, cap, width), bf16),
            pltpu.VMEM((rows, width), bf16),
            pltpu.VMEM((rows, kv_width), f32),
            pltpu.VMEM((rows, kv_width), f32),
            dma((len(args),)),
            dma((2 * bits,)),
            dma((2 * bits,)),
            dma((n_expert,)),
            dma((n_expert,)),
            dma((2,)),
            dma((bits,)),
            dma((bits,)),
            dma((n_expert,)),
            dma((n_expert,)),
            dma((3,)),
        ]
        outs = (
            jax.ShapeDtypeStruct((rows, width), bf16),
            jax.ShapeDtypeStruct((rows, kv_width), f32),
            jax.ShapeDtypeStruct((rows, kv_width), f32),
            jax.ShapeDtypeStruct(expert_out.shape, bf16),
        )
        anywhere = pl.BlockSpec(memory_space=pl.ANY)
        done = pl.pallas_call(
            functools.partial(body, n_context, n_expert),
            out_shape=outs,
            in_specs=[anywhere] * len(args),
            out_specs=(anywhere,) * 4,
            scratch_shapes=scratch,
            compiler_params=pltpu.CompilerParams(
                collective_id=0, has_side_effects=True, vmem_limit_bytes=62 * 1024 * 1024
            ),
        )(*args)
        return pl.pallas_call(
            finish,
            out_shape=outs,
            in_specs=[anywhere] * 4,
            out_specs=(anywhere,) * 4,
            scratch_shapes=[
                pltpu.VMEM((rows, width), bf16),
                pltpu.VMEM((rows, kv_width), f32),
                pltpu.VMEM((rows, kv_width), f32),
                pltpu.VMEM((n_expert, cap, width), bf16),
                dma((2, 3 + n_expert)),
            ],
            compiler_params=pltpu.CompilerParams(vmem_limit_bytes=62 * 1024 * 1024),
        )(*done)

    rows_spec = P(("groups", "context", "expert"), "tensor")
    expert_spec = P(("groups", "context"), "expert", None, None, "tensor")
    return jax.shard_map(
        local,
        mesh=mesh,
        in_specs=(
            rows_spec,
            rows_spec,
            rows_spec,
            rows_spec,
            expert_spec,
            P(("groups", "context", "expert"), None),
            P(("groups", "context", "expert"), None),
            P(("context", "expert"), None),
            P("groups"),
            P("groups", None),
            P("tensor"),
            P("tensor", None),
        ),
        out_specs=(rows_spec, rows_spec, rows_spec, expert_spec),
        check_vma=False,
    )
```

```python
import functools

import jax
import jax.numpy as jnp
from jax import lax
from jax.experimental import pallas as pl
from jax.experimental.pallas import tpu as pltpu
from jax.sharding import PartitionSpec as P

BLOCK = 128
HEAD = 128
LOSS_SCALE = 256
D = 2048
EPSILON = 1e-05
NEGATIVE = -1e30
LOG2E = 1.4426950408889634
MESH = pl.DeviceIdType.MESH
NT = (((1,), (1,)), ((), ()))
NN = (((1,), (0,)), ((), ()))
TN = (((0,), (0,)), ((), ()))


def dot(a, b, dims):
    return lax.dot_general(a, b, dims, preferred_element_type=jnp.float32)


def flipped(index, bit):
    step = 1 << bit
    return index + step * (1 - 2 * ((index // step) % 2))


def body(
    n_context,
    n_expert,
    q_hbm,
    k_hbm,
    v_hbm,
    r_hbm,
    x_hbm,
    routes_hbm,
    rw_hbm,
    pat_hbm,
    len_hbm,
    tea_hbm,
    gain_hbm,
    hw_hbm,
    gq_hbm,
    gk_hbm,
    gv_hbm,
    gx_hbm,
    q_v,
    r_v,
    kbuf,
    vbuf,
    xbuf,
    routes_v,
    rw_v,
    pat_s,
    len_v,
    tea_v,
    gain_v,
    hw_v,
    qst,
    pt_v,
    ptb_v,
    attn_v,
    hid_v,
    dost,
    hw3_v,
    ex_send,
    ex_recv,
    gsend,
    grecv,
    xsend,
    pick_v,
    put_v,
    gq_v,
    gk_v,
    gv_v,
    in_sem,
    kv_send_sem,
    kv_recv_sem,
    x_send_sem,
    x_recv_sem,
    ex_sem,
    g_send_sem,
    g_recv_sem,
    gx_send_sem,
    gx_recv_sem,
    out_sem,
):
    ctx = lax.axis_index("context")
    exp = lax.axis_index("expert")
    ten = lax.axis_index("tensor")
    shard = ctx * n_expert + exp
    e_bits = n_expert.bit_length() - 1
    c_bits = n_context.bit_length() - 1
    bits = e_bits + c_bits
    rows = q_v.shape[0]
    width = q_v.shape[1]
    kv_dev = kbuf.shape[2] // HEAD
    group = width // HEAD // kv_dev
    cap = xbuf.shape[1]
    span = (1 + bits) * BLOCK
    cats = hw_v.shape[0]
    turns = tea_v.shape[0]
    scale = HEAD ** (-0.5)

    def partner(bit):
        if bit < e_bits:
            return {"expert": flipped(exp, bit)}
        return {"context": flipped(ctx, bit - e_bits)}

    def mate(distance):
        index = exp
        for bit in range(e_bits):
            if distance >> bit & 1:
                index = flipped(index, bit)
        return index

    others = [{"expert": mate(off)} for off in range(1, n_expert)]
    peers = others + [partner(bit) for bit in range(e_bits, bits)] + [{"tensor": 1 - ten}]
    barrier = pltpu.get_barrier_semaphore()
    for peer in peers:
        pl.semaphore_signal(barrier, inc=1, device_id=peer, device_id_type=MESH)

    local_list = [
        (q_hbm, q_v),
        (k_hbm, kbuf.at[0]),
        (v_hbm, vbuf.at[0]),
        (r_hbm, r_v),
        (x_hbm.at[0, 0, exp], xbuf.at[0]),
        (routes_hbm, routes_v),
        (rw_hbm, rw_v),
        (pat_hbm, pat_s),
        (len_hbm, len_v),
        (tea_hbm, tea_v),
        (gain_hbm, gain_v),
        (hw_hbm, hw_v),
    ]
    local = [
        pltpu.make_async_copy(src, dst, in_sem.at[i]) for i, (src, dst) in enumerate(local_list)
    ]
    for copy in local:
        copy.start()
    pl.semaphore_wait(barrier, len(peers))

    kv_copies = []
    x_copies = []

    def send_kv(bit):
        for j, (src, dst) in enumerate(((k_hbm, kbuf), (v_hbm, vbuf))):
            copy = pltpu.make_async_remote_copy(
                src_ref=src,
                dst_ref=dst.at[1 + bit],
                send_sem=kv_send_sem.at[2 * bit + j],
                recv_sem=kv_recv_sem.at[2 * bit + j],
                device_id=partner(bit),
                device_id_type=MESH,
            )
            copy.start()
            kv_copies.append(copy)

    def send_x(off):
        copy = pltpu.make_async_remote_copy(
            src_ref=x_hbm.at[0, 0, mate(off)],
            dst_ref=xbuf.at[off],
            send_sem=x_send_sem.at[off],
            recv_sem=x_recv_sem.at[off],
            device_id=others[off - 1],
            device_id_type=MESH,
        )
        copy.start()
        x_copies.append(copy)

    far = list(range(e_bits))[::-1]
    for bit in far + list(range(e_bits, bits)):
        send_kv(bit)
    for off in range(n_expert - 1, 0, -1):
        send_x(off)
    for copy in local:
        copy.wait()

    lane = lax.broadcasted_iota(jnp.int32, (rows, 128), 1)
    name = lax.broadcasted_iota(jnp.int32, (128, rows), 0)
    row = lax.broadcasted_iota(jnp.int32, (rows, rows), 0)
    col = lax.broadcasted_iota(jnp.int32, (rows, rows), 1)
    member = jnp.zeros((128, rows), jnp.float32)
    weight = jnp.zeros((128, rows), jnp.float32)
    for k in range(routes_v.shape[0]):
        hit = routes_v[k : k + 1, :] == name
        member = member + jnp.where(hit, 1.0, 0.0)
        weight = weight + jnp.where(hit, rw_v[k : k + 1, :], 0.0)
    before = dot(
        member.astype(jnp.bfloat16), jnp.where(row < col, 1.0, 0.0).astype(jnp.bfloat16), NN
    )
    slot_row = jnp.where(member > 0, before, -1.0)
    slot = slot_row.T
    weight = weight.T
    cap_lane = lax.broadcasted_iota(jnp.int32, (rows, cap), 1).astype(jnp.float32)
    cap_row = lax.broadcasted_iota(jnp.int32, (cap, rows), 0).astype(jnp.float32)
    weight_cols = []
    for off in range(n_expert):
        mine = lane == mate(off)
        slot_col = jnp.sum(jnp.where(mine, slot, 0.0), axis=1, keepdims=True)
        weight_cols.append(jnp.sum(jnp.where(mine, weight, 0.0), axis=1, keepdims=True))
        one_row = jnp.sum(jnp.where(name == mate(off), slot_row, 0.0), axis=0, keepdims=True)
        pick_v[off] = jnp.where(slot_col == cap_lane, 1.0, 0.0).astype(jnp.bfloat16)
        put_v[off] = jnp.where(one_row == cap_row, 1.0, 0.0).astype(jnp.bfloat16)

    turn_row = lax.broadcasted_iota(jnp.int32, (turns, turns), 0)
    turn_col = lax.broadcasted_iota(jnp.int32, (turns, turns), 1)
    length_row = len_v[...].astype(jnp.float32)
    ends = jnp.sum(jnp.where(turn_col <= turn_row, length_row, 0.0), axis=1, keepdims=True)
    starts = jnp.sum(jnp.where(turn_col < turn_row, length_row, 0.0), axis=1, keepdims=True)
    position = (
        lax.broadcasted_iota(jnp.int32, (turns, rows), 1) + shard * rows
    ).astype(jnp.float32)
    turn_pick = jnp.where((starts <= position) & (position < ends), 1.0, 0.0)
    target = lax.dot_general(
        turn_pick,
        tea_v[...],
        TN,
        precision=lax.Precision.HIGHEST,
        preferred_element_type=jnp.float32,
    )

    hw = hw_v[...]
    hw_hi = hw.astype(jnp.bfloat16)
    hw_lo = (hw - hw_hi.astype(jnp.float32)).astype(jnp.bfloat16)
    hw3_v[...] = jnp.concatenate([hw_hi, hw_lo, hw_hi], axis=0)

    for g in range(kv_dev):
        for h in range(group):
            head = g * group + h
            qst[g, h * rows : (h + 1) * rows, :] = q_v[:, head * HEAD : (head + 1) * HEAD]

    for copy in kv_copies:
        copy.wait_recv()
    keep = [jnp.float32(1.0)]
    for bit in range(bits):
        other = flipped(exp, bit) + ctx * n_expert
        if bit >= e_bits:
            other = flipped(ctx, bit - e_bits) * n_expert + exp
        keep.append(pat_s[0, other].astype(jnp.float32))
    for g in range(kv_dev):
        lanes = slice(g * HEAD, (g + 1) * HEAD)
        parts = []
        for b in range(1 + bits):
            s = dot(kbuf[b, :, lanes], qst[g], NT)
            if b == 0:
                parts.append(s * (scale * LOG2E))
            else:
                parts.append(s * (keep[b] * (scale * LOG2E)) + (1.0 - keep[b]) * NEGATIVE)
        top_score = functools.reduce(
            jnp.maximum, [jnp.max(s, axis=0, keepdims=True) for s in parts]
        )
        parts = [jnp.exp2(s - top_score) for s in parts]
        total = functools.reduce(jnp.add, [jnp.sum(s, axis=0, keepdims=True) for s in parts])
        inverse = 1.0 / total
        for b in range(1 + bits):
            prob = parts[b] * inverse
            pt_v[g, b * BLOCK : (b + 1) * BLOCK, :] = prob
            ptb_v[g, b * BLOCK : (b + 1) * BLOCK, :] = prob.astype(jnp.bfloat16)
        value_set = vbuf[:, :, lanes].reshape(span, HEAD)
        out_t = dot(value_set, ptb_v[g], TN)
        for h in range(group):
            head = g * group + h
            attn_v[:, head * HEAD : (head + 1) * HEAD] = out_t[:, h * rows : (h + 1) * rows].T

    hid_v[...] = r_v[...].astype(jnp.float32) + attn_v[...]
    for off in range(n_expert):
        if off:
            x_copies[-off].wait_recv()
        hid_v[...] += weight_cols[off] * dot(pick_v[off], xbuf[off], NN)

    hidden = hid_v[...]
    gain = gain_v[...]
    square = jnp.sum(hidden * hidden, axis=1, keepdims=True)
    scaled = hidden * gain
    part_hi = scaled.astype(jnp.bfloat16)
    part_lo = (scaled - part_hi.astype(jnp.float32)).astype(jnp.bfloat16)
    first = dot(part_hi, hw3_v[: 2 * cats, :], NT)
    raw_part = first[:, :cats] + first[:, cats:] + dot(part_lo, hw3_v[:cats, :], NT)
    ex_send[...] = jnp.concatenate([raw_part, jnp.broadcast_to(square, (rows, 128 - cats))], axis=1)
    ex_copy = pltpu.make_async_remote_copy(
        src_ref=ex_send,
        dst_ref=ex_recv,
        send_sem=ex_sem.at[0],
        recv_sem=ex_sem.at[1],
        device_id={"tensor": 1 - ten},
        device_id_type=MESH,
    )
    ex_copy.start()
    ex_copy.wait()
    both = ex_send[...] + ex_recv[...]
    raw = both[:, :cats]
    rms = jnp.sqrt(both[:, cats : cats + 1] / D + EPSILON)
    inv = 1.0 / rms
    grad_logit = (jax.nn.sigmoid(raw * inv) - target) * LOSS_SCALE
    inner = jnp.sum(grad_logit * raw, axis=1, keepdims=True)
    gl_hi = grad_logit.astype(jnp.bfloat16)
    gl_lo = (grad_logit - gl_hi.astype(jnp.float32)).astype(jnp.bfloat16)
    normed = dot(jnp.concatenate([gl_hi, gl_hi, gl_lo], axis=1), hw3_v[...], NN)
    grad_hidden = gain * normed * inv - hidden * (inner / (D * rms * rms * rms))
    hid_v[...] = grad_hidden

    gx_copies = []
    for off in range(n_expert - 1, -1, -1):
        weighted = (weight_cols[off] * hid_v[...]).astype(jnp.bfloat16)
        xsend[off] = dot(put_v[off], weighted, NN).astype(jnp.bfloat16)
        if off:
            copy = pltpu.make_async_remote_copy(
                src_ref=xsend.at[off],
                dst_ref=gx_hbm.at[0, 0, exp],
                send_sem=gx_send_sem.at[off],
                recv_sem=gx_recv_sem.at[off],
                device_id=others[off - 1],
                device_id_type=MESH,
            )
        else:
            copy = pltpu.make_async_copy(xsend.at[0], gx_hbm.at[0, 0, exp], gx_send_sem.at[0])
        copy.start()
        gx_copies.append(copy)

    for g in range(kv_dev):
        for h in range(group):
            head = g * group + h
            dost[g, h * rows : (h + 1) * rows, :] = hid_v[
                :, head * HEAD : (head + 1) * HEAD
            ].astype(jnp.bfloat16)
    for g in range(kv_dev):
        lanes = slice(g * HEAD, (g + 1) * HEAD)
        key_set = kbuf[:, :, lanes].reshape(span, HEAD)
        value_set = vbuf[:, :, lanes].reshape(span, HEAD)
        grad_prob = dot(value_set, dost[g], NT)
        prob = pt_v[g]
        delta = jnp.sum(prob * grad_prob, axis=0, keepdims=True)
        score = (prob * (grad_prob - delta) * scale).astype(jnp.bfloat16)
        key_grad = dot(score, qst[g], NN)
        value_grad = dot(ptb_v[g], dost[g], NN)
        gk_v[:, lanes] = key_grad[:BLOCK]
        gv_v[:, lanes] = value_grad[:BLOCK]
        for b in range(bits):
            rows_b = slice((1 + b) * BLOCK, (2 + b) * BLOCK)
            gsend[b, 0, :, lanes] = key_grad[rows_b].astype(jnp.bfloat16)
            gsend[b, 1, :, lanes] = value_grad[rows_b].astype(jnp.bfloat16)
        query_t = dot(key_set, score, TN)
        for h in range(group):
            head = g * group + h
            gq_v[:, head * HEAD : (head + 1) * HEAD] = query_t[:, h * rows : (h + 1) * rows].T.astype(
                jnp.bfloat16
            )
    g_copies = []
    for bit in far + list(range(e_bits, bits)):
        copy = pltpu.make_async_remote_copy(
            src_ref=gsend.at[bit],
            dst_ref=grecv.at[bit],
            send_sem=g_send_sem.at[bit],
            recv_sem=g_recv_sem.at[bit],
            device_id=partner(bit),
            device_id_type=MESH,
        )
        copy.start()
        g_copies.append(copy)
    gq_copy = pltpu.make_async_copy(gq_v, gq_hbm, out_sem.at[0])
    gq_copy.start()
    for i, bit in enumerate(far + list(range(e_bits, bits))):
        g_copies[i].wait_recv()
        gk_v[...] += grecv[bit, 0].astype(jnp.float32)
        gv_v[...] += grecv[bit, 1].astype(jnp.float32)
    gk_copy = pltpu.make_async_copy(gk_v, gk_hbm, out_sem.at[1])
    gk_copy.start()
    gv_copy = pltpu.make_async_copy(gv_v, gv_hbm, out_sem.at[2])
    gv_copy.start()
    for copy in kv_copies + x_copies + g_copies:
        copy.wait_send()
    for copy in gx_copies:
        copy.wait()
    gq_copy.wait()
    gk_copy.wait()
    gv_copy.wait()


def finish(*refs):
    sources, results, held, sems = refs[:4], refs[4:8], refs[8:12], refs[12]
    pieces = list(zip(sources[:3], results[:3], held[:3]))
    for i in range(held[3].shape[0]):
        pieces.append((sources[3].at[0, 0, i], results[3].at[0, 0, i], held[3].at[i]))
    loads = [
        pltpu.make_async_copy(src, mid, sems.at[0, i]) for i, (src, _, mid) in enumerate(pieces)
    ]
    stores = [
        pltpu.make_async_copy(mid, dst, sems.at[1, i]) for i, (_, dst, mid) in enumerate(pieces)
    ]
    for load in loads:
        load.start()
    for load, store in zip(loads, stores):
        load.wait()
        store.start()
    for store in stores:
        store.wait()


def solution(mesh):
    n_context = mesh.shape["context"]
    n_expert = mesh.shape["expert"]
    bits = (n_context * n_expert).bit_length() - 1

    def local(
        queries,
        keys,
        values,
        resid,
        expert_out,
        routes,
        route_weights,
        pattern,
        lengths,
        teacher,
        gain,
        head_weight,
    ):
        rows, width = queries.shape
        kv_width = keys.shape[1]
        kv_dev = kv_width // HEAD
        group = width // HEAD // kv_dev
        span = (1 + bits) * BLOCK
        cap = expert_out.shape[3]
        lengths = lengths.reshape(1, -1)
        gain = gain.reshape(1, -1)
        cats = head_weight.shape[1]
        head_weight, routes, route_weights = head_weight.T, routes.T, route_weights.T
        bf16, f32 = jnp.bfloat16, jnp.float32
        dma = pltpu.SemaphoreType.DMA
        args = (
            queries,
            keys,
            values,
            resid,
            expert_out,
            routes,
            route_weights,
            pattern,
            lengths,
            teacher,
            gain,
            head_weight,
        )
        scratch = [
            pltpu.VMEM((rows, width), bf16),
            pltpu.VMEM((rows, width), bf16),
            pltpu.VMEM((1 + bits, rows, kv_width), bf16),
            pltpu.VMEM((1 + bits, rows, kv_width), bf16),
            pltpu.VMEM((n_expert, cap, width), bf16),
            pltpu.VMEM(routes.shape, jnp.int32),
            pltpu.VMEM(route_weights.shape, f32),
            pltpu.SMEM(pattern.shape, jnp.int32),
            pltpu.VMEM(lengths.shape, jnp.int32),
            pltpu.VMEM(teacher.shape, f32),
            pltpu.VMEM(gain.shape, f32),
            pltpu.VMEM(head_weight.shape, f32),
            pltpu.VMEM((kv_dev, group * rows, HEAD), bf16),
            pltpu.VMEM((kv_dev, span, group * rows), f32),
            pltpu.VMEM((kv_dev, span, group * rows), bf16),
            pltpu.VMEM((rows, width), f32),
            pltpu.VMEM((rows, width), f32),
            pltpu.VMEM((kv_dev, group * rows, HEAD), bf16),
            pltpu.VMEM((3 * cats, width), bf16),
            pltpu.VMEM((rows, 128), f32),
            pltpu.VMEM((rows, 128), f32),
            pltpu.VMEM((bits, 2, rows, kv_width), bf16),
            pltpu.VMEM((bits, 2, rows, kv_width), bf16),
            pltpu.VMEM((n_expert, cap, width), bf16),
            pltpu.VMEM((n_expert, rows, cap), bf16),
            pltpu.VMEM((n_expert, cap, rows), bf16),
            pltpu.VMEM((rows, width), bf16),
            pltpu.VMEM((rows, kv_width), f32),
            pltpu.VMEM((rows, kv_width), f32),
            dma((len(args),)),
            dma((2 * bits,)),
            dma((2 * bits,)),
            dma((n_expert,)),
            dma((n_expert,)),
            dma((2,)),
            dma((bits,)),
            dma((bits,)),
            dma((n_expert,)),
            dma((n_expert,)),
            dma((3,)),
        ]
        outs = (
            jax.ShapeDtypeStruct((rows, width), bf16),
            jax.ShapeDtypeStruct((rows, kv_width), f32),
            jax.ShapeDtypeStruct((rows, kv_width), f32),
            jax.ShapeDtypeStruct(expert_out.shape, bf16),
        )
        anywhere = pl.BlockSpec(memory_space=pl.ANY)
        done = pl.pallas_call(
            functools.partial(body, n_context, n_expert),
            out_shape=outs,
            in_specs=[anywhere] * len(args),
            out_specs=(anywhere,) * 4,
            scratch_shapes=scratch,
            compiler_params=pltpu.CompilerParams(
                collective_id=0, has_side_effects=True, vmem_limit_bytes=62 * 1024 * 1024
            ),
        )(*args)
        return pl.pallas_call(
            finish,
            out_shape=outs,
            in_specs=[anywhere] * 4,
            out_specs=(anywhere,) * 4,
            scratch_shapes=[
                pltpu.VMEM((rows, width), bf16),
                pltpu.VMEM((rows, kv_width), f32),
                pltpu.VMEM((rows, kv_width), f32),
                pltpu.VMEM((n_expert, cap, width), bf16),
                dma((2, 3 + n_expert)),
            ],
            compiler_params=pltpu.CompilerParams(vmem_limit_bytes=62 * 1024 * 1024),
        )(*done)

    rows_spec = P(("groups", "context", "expert"), "tensor")
    expert_spec = P(("groups", "context"), "expert", None, None, "tensor")
    return jax.shard_map(
        local,
        mesh=mesh,
        in_specs=(
            rows_spec,
            rows_spec,
            rows_spec,
            rows_spec,
            expert_spec,
            P(("groups", "context", "expert"), None),
            P(("groups", "context", "expert"), None),
            P(("context", "expert"), None),
            P("groups"),
            P("groups", None),
            P("tensor"),
            P("tensor", None),
        ),
        out_specs=(rows_spec, rows_spec, rows_spec, expert_spec),
        check_vma=False,
    )
```
